512 devices in a mesh: gx: 16 (over y, x), gy: 32 (over z, core).
Axes of the slice: x: 4, y: 4, z: 16, core: 2. Of those that a mesh axis runs over, the one named last changes fastest.
Arguments:
- tiles: bfloat16 [256, 96, 128, 128], P('gx', 'gy'), may hold values from 0.0099487305 to 1
- tile_cols: int32 [256, 96], P('gx', 'gy'), may hold values from 0 to 7
- row_counts: int32 [256, 32], P('gx', 'gy'), may hold values from 0 to 3
- start_block: bfloat16 [32768, 128], P('gx'), may hold values from -6 to 6
Outputs:
- vectors: bfloat16 [32768, 128], P(('gx', 'gy'))
- col_scales: float32 [2, 128], replicated
The draws below stay inside these ranges and needn't reach their ends.
Inputs may be any that keep to these rules, and one draw needn't show every extreme that they name: `tile_cols`: a column tile inside the slot's block of columns. `row_counts`: slots at or past the count are ignored.
All inputs are finite; a program needn't handle non-finite values.
Results may differ from the reference program's by a relative error of at most 0.0065.
Values may be sent and summed in bfloat16 or wider, within the bound.
No kernel may reach another device: no remote copies, remote signals or barrier semaphores. Data moves between devices by JAX's collectives and lax.ppermute only.
A program may use at most 64 MiB of HBM per device.

```python
import math
import jax
import jax.numpy as jnp
import numpy as np
from jax import lax

TILE = 128
K = 128
RT = 16
MAXT = 3
ROWTILES = 256
CT = 8
NODES = 32768
N_GX = 16
N_GY = 32


def with_ends(values, stream_key, low, high):
    extent = values.shape
    index_at = [jax.random.randint(jax.random.fold_in(stream_key, axis), (), 0, extent[axis]) for axis in range(len(extent))]
    values = values.at[tuple(index_at)].set(low)
    longest = extent.index(max(extent))
    index_at[longest] = (index_at[longest] + 1) % extent[longest]
    return values.at[tuple(index_at)].set(high)


def steps_of(stream_key, extent, pieces, low, top_value):
    def one(dim, shards_of):
        draws = jax.random.uniform(jax.random.fold_in(jax.random.fold_in(stream_key, 6), dim), (shards_of,), jnp.float32, low / len(pieces), top_value / len(pieces))
        return jnp.repeat(jnp.exp(draws), extent[dim] // shards_of).reshape((-1,) + (1,) * (len(extent) - dim - 1))

    loudness = one(*pieces[0])
    for cut in pieces[1:]:
        loudness = loudness * one(*cut)
    return loudness


def rank_table(amount, skew):
    weights = [(1 << 20) // math.isqrt(grade ** skew) + 1 for grade in range(1, amount + 1)]
    scale = 1 + sum(weights) // (1 << 30)
    return np.cumsum(np.array([max(1, weight // scale) for weight in weights]))


def ranked(own_key, extent, amount, lean):
    table = rank_table(amount, lean)
    lot = jax.random.randint(jax.random.fold_in(own_key, 1), extent, 0, int(table[amount - 1]))
    standing = jnp.searchsorted(jnp.asarray(table, jnp.int32), lot, side="right")
    return jax.random.permutation(jax.random.fold_in(own_key, 2), amount)[standing].astype(jnp.int32)


def centred(rng, extent, deviation, most, cuts=(), kind=jnp.bfloat16):
    gain = steps_of(rng, extent, cuts, -0.22, 0.18) if cuts else 1.0
    entries = jax.random.normal(rng, extent, jnp.float32) * deviation * gain
    return jnp.minimum(jnp.maximum(entries, -most), most).astype(kind)


def setup_inputs(seed: int = 0) -> dict:
    seeds = jax.random.split(jax.random.key(seed), 5)
    return {
        "tiles": jnp.clip(jnp.exp(math.log(1.0) - 4.61031033 * jax.random.uniform(seeds[0], (ROWTILES, N_GY * MAXT, TILE, TILE), jnp.float32) ** steps_of(seeds[0], (ROWTILES, N_GY * MAXT, TILE, TILE), ((0, 16), (1, 32)), -0.2, 0.2)), 0.0099487305, 1.0).astype(jnp.bfloat16),
        "tile_cols": with_ends(jax.random.randint(seeds[1], (ROWTILES, N_GY * MAXT), 0, CT), jax.random.fold_in(seeds[1], 1), 0, CT - 1).astype(jnp.int32),
        "row_counts": with_ends(ranked(seeds[2], (ROWTILES, N_GY), MAXT + 1, 2), jax.random.fold_in(seeds[2], 3), 0, MAXT).astype(jnp.int32),
        "start_block": centred(seeds[3], (NODES, K), 1.0, 6.0, ((0, 16),)),
    }


def apply_graph(tiles, tile_cols, row_counts, upd):
    row_tiles = tiles.shape[0]
    col_tiles = RT * N_GX // N_GY
    slots = jnp.arange(MAXT)

    def one_block(index, total):
        index = jnp.asarray(index).astype(jnp.int32)
        block_tiles = lax.dynamic_slice_in_dim(tiles, (index * MAXT).astype(jnp.int32), MAXT, 1).astype(jnp.float32)
        block_cols = lax.dynamic_slice_in_dim(tile_cols, (index * MAXT).astype(jnp.int32), MAXT, 1)
        counts = lax.dynamic_slice_in_dim(row_counts, index, 1, 1)
        masks = (slots[None, :] < counts).astype(jnp.float32)
        column = lax.dynamic_slice_in_dim(upd, (index * col_tiles * TILE).astype(jnp.int32), col_tiles * TILE, 0)
        column = column.reshape(col_tiles, TILE, K).astype(jnp.float32)
        picked = column[block_cols] * masks[:, :, None, None]
        return total + jnp.einsum('rsab,rsbk->rak', block_tiles, picked)
    total = lax.fori_loop(0, N_GY, one_block, jnp.zeros((row_tiles, TILE, K), jnp.float32))
    return total.reshape(row_tiles * TILE, K)

def row_degree(tiles, row_counts):
    slots = jnp.arange(MAXT)

    def one_block(index, total):
        index = jnp.asarray(index).astype(jnp.int32)
        block_tiles = lax.dynamic_slice_in_dim(tiles, (index * MAXT).astype(jnp.int32), MAXT, 1).astype(jnp.float32)
        counts = lax.dynamic_slice_in_dim(row_counts, index, 1, 1)
        masks = (slots[None, :] < counts).astype(jnp.float32)
        return total + jnp.einsum('rsab,rs->ra', block_tiles, masks)
    total = lax.fori_loop(0, N_GY, one_block, jnp.zeros((tiles.shape[0], TILE), jnp.float32))
    return 1.0 + total.reshape(-1)

def reference(tiles, tile_cols, row_counts, start_block):
    nodes = tiles.shape[0] * TILE
    scale = 1.0 / jnp.sqrt(row_degree(tiles, row_counts))
    upd = (scale[:, None] * start_block.astype(jnp.float32)).astype(jnp.bfloat16)
    scales = []
    vectors = upd
    for step in range(2):
        partial_value = apply_graph(tiles, tile_cols, row_counts, upd)
        mixed = scale[:, None] * (partial_value + upd.astype(jnp.float32))
        spread = jnp.sqrt(lax.optimization_barrier(jnp.sum(mixed * mixed, axis=0)) / nodes + 1e-06)
        scales.append(spread)
        normed = mixed / spread
        if step == 0:
            upd = (scale[:, None] * normed).astype(jnp.bfloat16)
        else:
            vectors = normed.astype(jnp.bfloat16)
    return (vectors, jnp.stack(scales))
```

```python
import jax
import jax.numpy as jnp
from jax import lax
from jax.experimental import pallas as pl
from jax.experimental.pallas import tpu as pltpu
from jax.sharding import Mesh
from jax.sharding import PartitionSpec as P

GX = ("gx_0", "gx_1")
GY = ("gy_0", "gy_1")
EVERY = ("gx_0", "gx_1", "gy_0", "gy_1")
Z = "gy_0"
CORE = "gy_1"
PLANE = ("gx_0", "gx_1", "gy_1")


def exchange(array, axis):
    return lax.all_to_all(array, axis, 0, 0, tiled=True)


def from_everyone(array, axis):
    peers = lax.axis_size(axis)
    return exchange(jnp.broadcast_to(array[None], (peers, *array.shape)), axis)


def transpose_planes(array):
    n = lax.axis_size(GX)
    perm = [
        ((i * n + z) * 2 + c, (z * n + i) * 2 + c)
        for i in range(n)
        for z in range(n)
        for c in range(2)
    ]
    return lax.ppermute(array, EVERY, perm)


def row_sum_kernel(counts, tiles, out):
    row_tiles, slots, side, _ = tiles.shape
    for r in range(row_tiles):
        wide = jnp.concatenate([tiles[r, s] for s in range(slots)], axis=1)
        slot = lax.broadcasted_iota(jnp.int32, (8, slots * side), 1) // side
        live = jnp.where(slot < counts[r, 0], 1.0, 0.0).astype(tiles.dtype)
        sums = lax.dot_general(
            live, wide, (((1,), (1,)), ((), ())), preferred_element_type=jnp.float32
        )
        out[r : r + 1] = sums[0:1]


def pick(cols, counts, column, r, slots, side):
    parts = []
    for s in range(slots):
        start = pl.multiple_of(cols[r, s] * side, side)
        part = column[pl.ds(start, side), :]
        parts.append(jnp.where(s < counts[r, 0], part, jnp.zeros_like(part)))
    return jnp.concatenate(parts, axis=0)


def first_kernel(place, cols, counts, tiles, start, scale, mine, other, column):
    row_tiles, slots, side, _ = tiles.shape
    half = row_tiles // 2
    spread = jnp.transpose(scale[...])
    for t in range(half):
        rows = slice(t * side, (t + 1) * side)
        value = start[rows, :].astype(jnp.float32) * spread[:, t : t + 1]
        column[rows, :] = value.astype(column.dtype)
    for out, core in ((other, 1 - place[0]), (mine, place[0])):
        for t in range(half):
            r = core * half + t
            wide = jnp.concatenate([tiles[r, s] for s in range(slots)], axis=1)
            out[t * side : (t + 1) * side, :] = jnp.dot(
                wide,
                pick(cols, counts, column, r, slots, side),
                preferred_element_type=jnp.float32,
            )


def second_kernel(place, cols, counts, tiles, column, mine, other):
    row_tiles, slots, side, _ = tiles.shape
    half = row_tiles // 2
    share = side // 2
    core = place[0]
    for r in range(row_tiles):
        picked = pick(cols, counts, column, r, slots, side)
        diagonal = (place[1] == place[2]) & (core == r // half)
        for out, part in ((other, 1 - core), (mine, core)):
            rows = pl.ds(pl.multiple_of(part * share, share), share)
            wide = jnp.concatenate([tiles[r, s, rows, :] for s in range(slots)], axis=1)
            own = column[pl.ds((r % half) * side + part * share, share), :]
            value = jnp.dot(wide, picked, preferred_element_type=jnp.float32)
            value = value + jnp.where(diagonal, own.astype(jnp.float32), 0.0)
            out[r * share : (r + 1) * share, :] = value


SMEM = pl.BlockSpec(memory_space=pltpu.SMEM)
VMEM = pl.BlockSpec(memory_space=pltpu.VMEM)
PARAMS = pltpu.CompilerParams(vmem_limit_bytes=24 << 20)


def on_device(tiles, tile_cols, row_counts, start_block):
    row_tiles, slot_count, side, _ = tiles.shape
    width = start_block.shape[1]
    groups = lax.axis_size(GX)
    half_tiles = row_tiles // 2
    local_rows = row_tiles * side
    half_rows = local_rows // 2
    share = half_rows // groups
    nodes = local_rows * groups
    core = lax.axis_index(CORE)
    line = lax.axis_index(GX)
    plane = lax.axis_index(Z)
    f32, bf16 = jnp.float32, jnp.bfloat16

    start_col = transpose_planes(
        lax.dynamic_slice_in_dim(start_block, core * half_rows, half_rows, 0)
    )

    place = jnp.stack([core, line, plane]).astype(jnp.int32)
    row_sums = pl.pallas_call(
        row_sum_kernel,
        out_shape=jax.ShapeDtypeStruct((row_tiles, side), f32),
        in_specs=[SMEM, VMEM],
        out_specs=VMEM,
        compiler_params=PARAMS,
    )(row_counts, tiles)

    sent = jnp.broadcast_to(row_sums[None], (2 * groups, row_tiles, side))
    got = exchange(sent, PLANE).reshape(groups, 2, row_tiles, side).sum(axis=1)
    of_half = lax.dynamic_slice_in_dim(got, core * half_tiles, half_tiles, 1)
    of_line = lax.dynamic_index_in_dim(got, line, 0, keepdims=False)[:, None, :]
    both = exchange(jnp.concatenate([of_half, of_line], axis=1), Z).sum(axis=0)
    scale_all = 1.0 / jnp.sqrt(1.0 + both)
    scale_col = scale_all[:half_tiles]
    scale_own = lax.dynamic_slice_in_dim(scale_all[half_tiles], core * share, share, 0)
    scale_seg = lax.dynamic_slice_in_dim(
        scale_col.reshape(half_rows), line * share, share, 0
    )

    halves = [jax.ShapeDtypeStruct((half_rows, width), f32)] * 2

    def pair_sum(mine, other):
        return mine + lax.ppermute(other, CORE, [(0, 1), (1, 0)])

    pair = pair_sum(
        *pl.pallas_call(
            first_kernel,
            out_shape=halves,
            in_specs=[SMEM] * 3 + [VMEM] * 3,
            out_specs=[VMEM] * 2,
            scratch_shapes=[pltpu.VMEM((half_rows, width), bf16)],
            compiler_params=PARAMS,
        )(place, tile_cols, row_counts, tiles, start_col, scale_col)
    )
    chunks = pair.astype(bf16).reshape(groups, share, width)
    product = exchange(exchange(chunks, GX), Z).astype(f32).sum(axis=0)
    u_seg = lax.dynamic_slice_in_dim(start_col, line * share, share, 0).astype(f32)
    u_seg = (scale_seg[:, None] * u_seg).astype(bf16).astype(f32)
    w1 = scale_seg[:, None] * (product + u_seg)
    squares1 = jnp.sum(w1 * w1, axis=0)

    v_seg = (scale_seg[:, None] * w1).astype(bf16)
    v = from_everyone(v_seg, GX).reshape(half_rows, width)
    pair = pair_sum(
        *pl.pallas_call(
            second_kernel,
            out_shape=halves,
            in_specs=[SMEM] * 3 + [VMEM] * 2,
            out_specs=[VMEM] * 2,
            compiler_params=PARAMS,
        )(place, tile_cols, row_counts, tiles, v)
    ).reshape(row_tiles, share, width)
    product = exchange(pair.astype(bf16), Z).astype(f32).sum(axis=0)
    w2 = scale_own[:, None] * product
    squares2 = jnp.sum(w2 * w2, axis=0)

    squares = jnp.stack([squares1, squares2])
    squares = from_everyone(squares, PLANE).sum(axis=0)
    squares = from_everyone(squares, Z).sum(axis=0)
    spread1 = jnp.sqrt(squares[0] / nodes + 1e-06)
    spread2 = jnp.sqrt(squares[1] / (spread1 * spread1) / nodes + 1e-06)
    vectors = (w2 / (spread1 * spread2)).astype(bf16)
    return (vectors, jnp.stack([spread1, spread2]))


def solution(mesh):
    torus = Mesh(mesh.devices.reshape(4, 4, 16, 2), EVERY)
    placed = (P(GX, GY, None, None), P(GX, GY), P(GX, GY), P(GX, None))
    return jax.shard_map(
        on_device,
        mesh=torus,
        in_specs=placed,
        out_specs=(P(EVERY, None), P()),
        check_vma=False,
    )
```

```python
import jax
import jax.numpy as jnp
from jax import lax
from jax.experimental import pallas as pl
from jax.experimental.pallas import tpu as pltpu
from jax.sharding import Mesh
from jax.sharding import PartitionSpec as P

GX = ("gx_0", "gx_1")
GY = ("gy_0", "gy_1")
EVERY = ("gx_0", "gx_1", "gy_0", "gy_1")
Z = "gy_0"
CORE = "gy_1"
PLANE = ("gx_0", "gx_1", "gy_1")


def exchange(array, axis):
    return lax.all_to_all(array, axis, 0, 0, tiled=True)


def from_everyone(array, axis):
    peers = lax.axis_size(axis)
    return exchange(jnp.broadcast_to(array[None], (peers, *array.shape)), axis)


def row_sum_kernel(counts, tiles, out):
    row_tiles, slots, side, _ = tiles.shape
    for r in range(row_tiles):
        wide = jnp.concatenate([tiles[r, s] for s in range(slots)], axis=1)
        slot = lax.broadcasted_iota(jnp.int32, (8, slots * side), 1) // side
        live = jnp.where(slot < counts[r, 0], 1.0, 0.0).astype(tiles.dtype)
        sums = lax.dot_general(
            live, wide, (((1,), (1,)), ((), ())), preferred_element_type=jnp.float32
        )
        out[r : r + 1] = sums[0:1]


def pick(cols, counts, column, r, slots, side):
    parts = []
    for s in range(slots):
        start = pl.multiple_of(cols[r, s] * side, side)
        part = column[pl.ds(start, side), :]
        parts.append(jnp.where(s < counts[r, 0], part, jnp.zeros_like(part)))
    return jnp.concatenate(parts, axis=0)


def first_kernel(place, cols, counts, tiles, column, mine, other):
    row_tiles, slots, side, _ = tiles.shape
    half = row_tiles // 2
    for out, core in ((other, 1 - place[0]), (mine, place[0])):
        for t in range(half):
            r = core * half + t
            wide = jnp.concatenate([tiles[r, s] for s in range(slots)], axis=1)
            out[t * side : (t + 1) * side, :] = jnp.dot(
                wide,
                pick(cols, counts, column, r, slots, side),
                preferred_element_type=jnp.float32,
            )


def second_kernel(place, cols, counts, tiles, column, mine, other):
    row_tiles, slots, side, _ = tiles.shape
    half = row_tiles // 2
    share = side // 2
    core = place[0]
    for r in range(row_tiles):
        picked = pick(cols, counts, column, r, slots, side)
        diagonal = (place[1] == place[2]) & (core == r // half)
        for out, part in ((other, 1 - core), (mine, core)):
            rows = pl.ds(pl.multiple_of(part * share, share), share)
            wide = jnp.concatenate([tiles[r, s, rows, :] for s in range(slots)], axis=1)
            own = column[pl.ds((r % half) * side + part * share, share), :]
            value = jnp.dot(wide, picked, preferred_element_type=jnp.float32)
            value = value + jnp.where(diagonal, own.astype(jnp.float32), 0.0)
            out[r * share : (r + 1) * share, :] = value


SMEM = pl.BlockSpec(memory_space=pltpu.SMEM)
VMEM = pl.BlockSpec(memory_space=pltpu.VMEM)
PARAMS = pltpu.CompilerParams(vmem_limit_bytes=24 << 20)


def on_device(tiles, tile_cols, row_counts, start_block):
    row_tiles, slot_count, side, _ = tiles.shape
    width = start_block.shape[1]
    groups = lax.axis_size(GX)
    half_tiles = row_tiles // 2
    local_rows = row_tiles * side
    half_rows = local_rows // 2
    share = half_rows // groups
    nodes = local_rows * groups
    core = lax.axis_index(CORE)
    line = lax.axis_index(GX)
    plane = lax.axis_index(Z)
    f32, bf16 = jnp.float32, jnp.bfloat16

    place = jnp.stack([core, line, plane]).astype(jnp.int32)
    row_sums = pl.pallas_call(
        row_sum_kernel,
        out_shape=jax.ShapeDtypeStruct((row_tiles, side), f32),
        in_specs=[SMEM, VMEM],
        out_specs=VMEM,
        compiler_params=PARAMS,
    )(row_counts, tiles)

    def swapped(array):
        return lax.ppermute(array, CORE, [(0, 1), (1, 0)])

    row_sums = row_sums + swapped(row_sums)
    start_half = lax.dynamic_slice_in_dim(start_block, core * half_rows, half_rows, 0)
    part = lax.dynamic_slice_in_dim(row_sums, core * half_tiles, half_tiles, 0)
    part = jnp.repeat(part, 2, axis=0)
    high = lax.reduce_precision(part, 8, 7)
    middle = lax.reduce_precision(part - high, 8, 7)
    terms = jnp.stack([high, middle, part - high - middle], axis=1).astype(bf16)
    terms = jnp.pad(terms, ((0, 0), (0, 13), (0, 0)))
    sent = [start_half.reshape(groups, share, width), terms]
    got = exchange(jnp.concatenate(sent, axis=1), GX)
    start_seg = lax.dynamic_index_in_dim(got, plane, 0, keepdims=False)[:share]
    part = got[:, share : share + 3].astype(f32).sum(axis=1)

    degree = 1.0 + exchange(jnp.stack([part, row_sums], axis=1), Z).sum(axis=0)
    scale = 1.0 / jnp.sqrt(degree)
    scale_seg = lax.dynamic_slice_in_dim(scale[0], line % 2 * share, share, 0)
    scale_own = lax.dynamic_slice_in_dim(scale[1], core * share, share, 0)

    halves = [jax.ShapeDtypeStruct((half_rows, width), f32)] * 2

    def pair_sum(mine, other):
        return mine + swapped(other)

    u_seg = (scale_seg[:, None] * start_seg.astype(f32)).astype(bf16)
    u = from_everyone(u_seg, GX).reshape(half_rows, width)
    pair = pair_sum(
        *pl.pallas_call(
            first_kernel,
            out_shape=halves,
            in_specs=[SMEM] * 3 + [VMEM] * 2,
            out_specs=[VMEM] * 2,
            compiler_params=PARAMS,
        )(place, tile_cols, row_counts, tiles, u)
    )
    chunks = pair.astype(bf16).reshape(groups, share, width)
    product = exchange(exchange(chunks, GX), Z).astype(f32).sum(axis=0)
    w1 = scale_seg[:, None] * (product + u_seg.astype(f32))
    squares1 = jnp.sum(w1 * w1, axis=0)

    v_seg = (scale_seg[:, None] * w1).astype(bf16)
    v = from_everyone(v_seg, GX).reshape(half_rows, width)
    pair = pair_sum(
        *pl.pallas_call(
            second_kernel,
            out_shape=halves,
            in_specs=[SMEM] * 3 + [VMEM] * 2,
            out_specs=[VMEM] * 2,
            compiler_params=PARAMS,
        )(place, tile_cols, row_counts, tiles, v)
    ).reshape(row_tiles, share, width)
    product = exchange(pair.astype(bf16), Z).astype(f32).sum(axis=0)
    w2 = scale_own[:, None] * product
    squares2 = jnp.sum(w2 * w2, axis=0)

    squares = jnp.stack([squares1, squares2])
    squares = from_everyone(squares, PLANE).sum(axis=0)
    squares = from_everyone(squares, Z).sum(axis=0)
    spread1 = jnp.sqrt(squares[0] / nodes + 1e-06)
    spread2 = jnp.sqrt(squares[1] / (spread1 * spread1) / nodes + 1e-06)
    vectors = (w2 / (spread1 * spread2)).astype(bf16)
    return (vectors, jnp.stack([spread1, spread2]))


def solution(mesh):
    torus = Mesh(mesh.devices.reshape(4, 4, 16, 2), EVERY)
    placed = (P(GX, GY, None, None), P(GX, GY), P(GX, GY), P(GX, None))
    return jax.shard_map(
        on_device,
        mesh=torus,
        in_specs=placed,
        out_specs=(P(EVERY, None), P()),
        check_vma=False,
    )
```

```python
import jax
import jax.numpy as jnp
from jax import lax
from jax.experimental import pallas as pl
from jax.experimental.pallas import tpu as pltpu
from jax.sharding import Mesh
from jax.sharding import PartitionSpec as P

GX = ("gx_0", "gx_1")
GY = ("gy_0", "gy_1")
EVERY = ("gx_0", "gx_1", "gy_0", "gy_1")
Z = "gy_0"
CORE = "gy_1"
PLANE = ("gx_0", "gx_1", "gy_1")


def exchange(array, axis):
    return lax.all_to_all(array, axis, 0, 0, tiled=True)


def from_everyone(array, axis):
    peers = lax.axis_size(axis)
    return exchange(jnp.broadcast_to(array[None], (peers, *array.shape)), axis)


def row_sum_kernel(counts, tiles, out):
    here, slots, side, _ = tiles.shape
    step = pl.program_id(0)
    slot = lax.broadcasted_iota(jnp.int32, (8, slots * side), 1) // side
    for r in range(here):
        wide = jnp.concatenate([tiles[r, s] for s in range(slots)], axis=1)
        which = lax.broadcasted_iota(jnp.int32, counts.shape, 1) == step * here + r
        count = jnp.sum(jnp.where(which, counts[...], 0), axis=1, keepdims=True)
        live = jnp.where(slot < count, 1.0, 0.0).astype(tiles.dtype)
        sums = lax.dot_general(
            live, wide, (((1,), (1,)), ((), ())), preferred_element_type=jnp.float32
        )
        out[pl.ds(step * here + r, 1)] = sums[0:1]


def pick(cols, counts, column, r, slots, side):
    parts = []
    for s in range(slots):
        start = pl.multiple_of(cols[s, r] * side, side)
        part = column[pl.ds(start, side), :]
        live = s < counts[0, r]
        parts.append(jnp.where(live, part, jnp.zeros_like(part)))
    return jnp.concatenate(parts, axis=0)


def first_kernel(place, cols, counts, tiles, column, mine, other):
    row_tiles, slots, side, _ = tiles.shape
    half = row_tiles // 2
    for out, core in ((other, 1 - place[0]), (mine, place[0])):
        for t in range(half):
            r = core * half + t
            wide = jnp.concatenate([tiles[r, s] for s in range(slots)], axis=1)
            out[t * side : (t + 1) * side, :] = jnp.dot(
                wide,
                pick(cols, counts, column, r, slots, side),
                preferred_element_type=jnp.float32,
            )


def second_kernel(place, cols, counts, tiles, column, mine, other):
    row_tiles, slots, side, _ = tiles.shape
    half = row_tiles // 2
    share = side // 2
    core = place[0]
    for r in range(row_tiles):
        picked = pick(cols, counts, column, r, slots, side)
        diagonal = (place[1] == place[2]) & (core == r // half)
        for out, part in ((other, 1 - core), (mine, core)):
            rows = pl.ds(pl.multiple_of(part * share, share), share)
            wide = jnp.concatenate([tiles[r, s, rows, :] for s in range(slots)], axis=1)
            own = column[pl.ds((r % half) * side + part * share, share), :]
            value = jnp.dot(wide, picked, preferred_element_type=jnp.float32)
            value = value + jnp.where(diagonal, own.astype(jnp.float32), 0.0)
            out[r * share : (r + 1) * share, :] = value


SMEM = pl.BlockSpec(memory_space=pltpu.SMEM)
VMEM = pl.BlockSpec(memory_space=pltpu.VMEM)
PARAMS = pltpu.CompilerParams(vmem_limit_bytes=24 << 20)


def on_device(tiles, tile_cols, row_counts, start_block):
    row_tiles, slot_count, side, _ = tiles.shape
    width = start_block.shape[1]
    groups = lax.axis_size(GX)
    half_tiles = row_tiles // 2
    local_rows = row_tiles * side
    half_rows = local_rows // 2
    share = half_rows // groups
    nodes = local_rows * groups
    core = lax.axis_index(CORE)
    line = lax.axis_index(GX)
    plane = lax.axis_index(Z)
    f32, bf16 = jnp.float32, jnp.bfloat16

    place = jnp.stack([core, line, plane]).astype(jnp.int32)
    cols = tile_cols.T
    counts = row_counts.T
    steps = 2
    row_sums = pl.pallas_call(
        row_sum_kernel,
        grid=(steps,),
        out_shape=jax.ShapeDtypeStruct((row_tiles, side), f32),
        in_specs=[
            pl.BlockSpec((1, row_tiles), lambda g: (0, 0)),
            pl.BlockSpec(
                (row_tiles // steps, slot_count, side, side), lambda g: (g, 0, 0, 0)
            ),
        ],
        out_specs=pl.BlockSpec((row_tiles, side), lambda g: (0, 0)),
    )(counts, tiles)

    def swapped(array):
        return lax.ppermute(array, CORE, [(0, 1), (1, 0)])

    start_half = lax.dynamic_slice_in_dim(start_block, core * half_rows, half_rows, 0)
    part = row_sums.reshape(2, groups, share).transpose(1, 0, 2).reshape(groups, side)
    high = lax.reduce_precision(part, 8, 7)
    middle = lax.reduce_precision(part - high, 8, 7)
    terms = jnp.stack([high, middle, part - high - middle], axis=1).astype(bf16)
    terms = jnp.pad(terms, ((0, 0), (0, 13), (0, 0)))
    sent = [start_half.reshape(groups, share, width), terms]
    sent = jnp.concatenate(sent, axis=1)
    sent, place = lax.optimization_barrier((sent, place))
    got = exchange(sent, GX)
    start_seg = lax.dynamic_index_in_dim(got, plane, 0, keepdims=False)[:share]
    part = got[:, share : share + 3].astype(f32).sum(axis=1)

    both = jnp.concatenate([part[:, None], row_sums[:, None]], axis=2)
    both = jnp.repeat(both, 2, axis=0)
    degree = 1.0 + exchange(both, GY).sum(axis=(0, 1))
    scale = 1.0 / jnp.sqrt(degree)
    scale_seg = lax.dynamic_slice_in_dim(scale, core * share, share, 0)
    scale_own = lax.dynamic_slice_in_dim(scale, side + core * share, share, 0)

    halves = [jax.ShapeDtypeStruct((half_rows, width), f32)] * 2

    def pair_sum(mine, other):
        return mine + swapped(other)

    u_seg = (scale_seg[:, None] * start_seg.astype(f32)).astype(bf16)
    u = from_everyone(u_seg, GX).reshape(half_rows, width)
    pair = pair_sum(
        *pl.pallas_call(
            first_kernel,
            out_shape=halves,
            in_specs=[SMEM] * 3 + [VMEM] * 2,
            out_specs=[VMEM] * 2,
            compiler_params=PARAMS,
        )(place, cols, counts, tiles, u)
    )
    chunks = pair.astype(bf16).reshape(groups, share, width)
    product = exchange(exchange(chunks, GX), Z).astype(f32).sum(axis=0)
    w1 = scale_seg[:, None] * (product + u_seg.astype(f32))
    squares1 = jnp.sum(w1 * w1, axis=0)

    v_seg = (scale_seg[:, None] * w1).astype(bf16)
    v_seg, squares1, scale_own = lax.optimization_barrier((v_seg, squares1, scale_own))
    v = from_everyone(v_seg, GX).reshape(half_rows, width)
    pair = pair_sum(
        *pl.pallas_call(
            second_kernel,
            out_shape=halves,
            in_specs=[SMEM] * 3 + [VMEM] * 2,
            out_specs=[VMEM] * 2,
            compiler_params=PARAMS,
        )(place, cols, counts, tiles, v)
    ).reshape(row_tiles, share, width)
    product = exchange(pair.astype(bf16), Z).astype(f32).sum(axis=0)
    w2 = scale_own[:, None] * product
    squares2 = jnp.sum(w2 * w2, axis=0)

    squares = jnp.stack([squares1, squares2])
    squares = from_everyone(squares, PLANE).sum(axis=0)
    squares = from_everyone(squares, Z).sum(axis=0)
    spread1 = jnp.sqrt(squares[0] / nodes + 1e-06)
    spread2 = jnp.sqrt(squares[1] / (spread1 * spread1) / nodes + 1e-06)
    vectors = (w2 / (spread1 * spread2)).astype(bf16)
    return (vectors, jnp.stack([spread1, spread2]))


def solution(mesh):
    torus = Mesh(mesh.devices.reshape(4, 4, 16, 2), EVERY)
    placed = (P(GX, GY, None, None), P(GX, GY), P(GX, GY), P(GX, None))
    return jax.shard_map(
        on_device,
        mesh=torus,
        in_specs=placed,
        out_specs=(P(EVERY, None), P()),
        check_vma=False,
    )
```

```python
import jax
import jax.numpy as jnp
from jax import lax
from jax.experimental import pallas as pl
from jax.experimental.pallas import tpu as pltpu
from jax.sharding import Mesh
from jax.sharding import PartitionSpec as P

GX = ("gx_0", "gx_1")
GY = ("gy_0", "gy_1")
EVERY = ("gx_0", "gx_1", "gy_0", "gy_1")
Z = "gy_0"
CORE = "gy_1"
PLANE = ("gx_0", "gx_1", "gy_1")


def exchange(array, axis):
    return lax.all_to_all(array, axis, 0, 0, tiled=True)


def from_everyone(array, axis):
    peers = lax.axis_size(axis)
    return exchange(jnp.broadcast_to(array[None], (peers, *array.shape)), axis)


def row_sum_kernel(counts, tiles, out, terms, held):
    here, slots, side, _ = tiles.shape
    half = pl.program_id(0)
    slot = lax.broadcasted_iota(jnp.int32, (8, slots * side), 1) // side
    mine = lax.broadcasted_iota(jnp.int32, (1, side), 1) // (side // 2) == half
    row = lax.broadcasted_iota(jnp.int32, terms.shape[1:], 0)
    for t in range(here):
        wide = jnp.concatenate([tiles[t, s] for s in range(slots)], axis=1)
        which = lax.broadcasted_iota(jnp.int32, counts.shape, 1) == half * here + t
        count = jnp.sum(jnp.where(which, counts[...], 0), axis=1, keepdims=True)
        live = jnp.where(slot < count, 1.0, 0.0).astype(tiles.dtype)
        sums = lax.dot_general(
            live, wide, (((1,), (1,)), ((), ())), preferred_element_type=jnp.float32
        )[0:1]
        out[pl.ds(half * here + t, 1)] = sums
        turned = pltpu.roll(sums, side // 2, 1)
        for part in range(2):
            at = pl.ds(2 * t + part, 1)
            held[at] = jnp.where(
                mine, jnp.where(half == part, sums, turned), held[at]
            )

    @pl.when(half == 1)
    def _():
        for p in range(2 * here):
            value = held[p : p + 1]
            high = value.astype(terms.dtype).astype(jnp.float32)
            middle = (value - high).astype(terms.dtype).astype(jnp.float32)
            low = value - high - middle
            block = jnp.where(row == 1, middle, jnp.where(row == 2, low, 0.0))
            terms[p] = jnp.where(row == 0, high, block).astype(terms.dtype)


def pick(cols, counts, column, r, slots, side):
    parts = []
    for s in range(slots):
        start = pl.multiple_of(cols[s, r] * side, side)
        part = column[pl.ds(start, side), :]
        live = s < counts[0, r]
        parts.append(jnp.where(live, part, jnp.zeros_like(part)))
    return jnp.concatenate(parts, axis=0)


def first_kernel(place, cols, counts, tiles, column, mine, other):
    row_tiles, slots, side, _ = tiles.shape
    half = row_tiles // 2
    for out, core in ((other, 1 - place[0]), (mine, place[0])):
        for t in range(half):
            r = core * half + t
            wide = jnp.concatenate([tiles[r, s] for s in range(slots)], axis=1)
            out[t * side : (t + 1) * side, :] = jnp.dot(
                wide,
                pick(cols, counts, column, r, slots, side),
                preferred_element_type=jnp.float32,
            ).astype(out.dtype)


def second_kernel(place, cols, counts, tiles, column, mine, other):
    row_tiles, slots, side, _ = tiles.shape
    half = row_tiles // 2
    share = side // 2
    core = place[0]
    for r in range(row_tiles):
        picked = pick(cols, counts, column, r, slots, side)
        diagonal = (place[1] == place[2]) & (core == r // half)
        for out, part in ((other, 1 - core), (mine, core)):
            rows = pl.ds(pl.multiple_of(part * share, share), share)
            wide = jnp.concatenate([tiles[r, s, rows, :] for s in range(slots)], axis=1)
            own = column[pl.ds((r % half) * side + part * share, share), :]
            value = jnp.dot(wide, picked, preferred_element_type=jnp.float32)
            value = value + jnp.where(diagonal, own.astype(jnp.float32), 0.0)
            out[r * share : (r + 1) * share, :] = value.astype(out.dtype)


SMEM = pl.BlockSpec(memory_space=pltpu.SMEM)
VMEM = pl.BlockSpec(memory_space=pltpu.VMEM)
PARAMS = pltpu.CompilerParams(vmem_limit_bytes=24 << 20)


def on_device(tiles, tile_cols, row_counts, start_block):
    row_tiles, slot_count, side, _ = tiles.shape
    width = start_block.shape[1]
    groups = lax.axis_size(GX)
    half_tiles = row_tiles // 2
    local_rows = row_tiles * side
    half_rows = local_rows // 2
    share = half_rows // groups
    nodes = local_rows * groups
    core = lax.axis_index(CORE)
    line = lax.axis_index(GX)
    plane = lax.axis_index(Z)
    f32, bf16 = jnp.float32, jnp.bfloat16

    place = jnp.stack([core, line, plane]).astype(jnp.int32)
    cols = tile_cols.T
    counts = row_counts.T
    steps = 2
    row_sums, terms = pl.pallas_call(
        row_sum_kernel,
        grid=(steps,),
        out_shape=[
            jax.ShapeDtypeStruct((row_tiles, side), f32),
            jax.ShapeDtypeStruct((groups, 16, side), bf16),
        ],
        in_specs=[
            pl.BlockSpec((1, row_tiles), lambda g: (0, 0)),
            pl.BlockSpec(
                (row_tiles // steps, slot_count, side, side), lambda g: (g, 0, 0, 0)
            ),
        ],
        out_specs=[
            pl.BlockSpec((row_tiles, side), lambda g: (0, 0)),
            pl.BlockSpec((groups, 16, side), lambda g: (0, 0, 0)),
        ],
        scratch_shapes=[pltpu.VMEM((groups, side), f32)],
    )(counts, tiles)

    def swapped(array):
        return lax.ppermute(array, CORE, [(0, 1), (1, 0)])

    start_half = lax.dynamic_slice_in_dim(start_block, core * half_rows, half_rows, 0)
    sent = [start_half.reshape(groups, share, width), terms]
    sent = jnp.concatenate(sent, axis=1)
    at_seg = core * share
    at_own = side + at_seg
    sent, place, at_seg, at_own = lax.optimization_barrier((sent, place, at_seg, at_own))
    got = exchange(sent, GX)
    start_seg = lax.dynamic_index_in_dim(got, plane, 0, keepdims=False)[:share]
    part = got[:, share : share + 3].astype(f32).sum(axis=1)

    both = jnp.concatenate([part[:, None], row_sums[:, None]], axis=2)
    both = jnp.repeat(both, 2, axis=0)
    degree = 1.0 + exchange(both, GY).sum(axis=(0, 1))
    scale = 1.0 / jnp.sqrt(degree)
    scale_seg = lax.dynamic_slice_in_dim(scale, at_seg, share, 0)
    scale_own = lax.dynamic_slice_in_dim(scale, at_own, share, 0)

    halves = [jax.ShapeDtypeStruct((half_rows, width), t) for t in (f32, bf16)]

    def pair_sum(mine, other):
        return mine + swapped(other).astype(f32)

    u_seg = (scale_seg[:, None] * start_seg.astype(f32)).astype(bf16)
    u = from_everyone(u_seg, GX).reshape(half_rows, width)
    pair = pair_sum(
        *pl.pallas_call(
            first_kernel,
            out_shape=halves,
            in_specs=[SMEM] * 3 + [VMEM] * 2,
            out_specs=[VMEM] * 2,
            compiler_params=PARAMS,
        )(place, cols, counts, tiles, u)
    )
    chunks = pair.astype(bf16).reshape(groups, share, width)
    product = exchange(exchange(chunks, GX), Z).astype(f32).sum(axis=0)
    w1 = scale_seg[:, None] * (product + u_seg.astype(f32))
    squares1 = jnp.sum(w1 * w1, axis=0)

    v_seg = (scale_seg[:, None] * w1).astype(bf16)
    v_seg, squares1, scale_own = lax.optimization_barrier((v_seg, squares1, scale_own))
    v = from_everyone(v_seg, GX).reshape(half_rows, width)
    pair = pair_sum(
        *pl.pallas_call(
            second_kernel,
            out_shape=halves,
            in_specs=[SMEM] * 3 + [VMEM] * 2,
            out_specs=[VMEM] * 2,
            compiler_params=PARAMS,
        )(place, cols, counts, tiles, v)
    ).reshape(row_tiles, share, width)
    product = exchange(pair.astype(bf16), Z).astype(f32).sum(axis=0)
    w2 = scale_own[:, None] * product
    squares2 = jnp.sum(w2 * w2, axis=0)

    squares = jnp.stack([squares1, squares2])
    squares = from_everyone(squares, PLANE).sum(axis=0)
    squares = from_everyone(squares, Z).sum(axis=0)
    spread1 = jnp.sqrt(squares[0] / nodes + 1e-06)
    spread2 = jnp.sqrt(squares[1] / (spread1 * spread1) / nodes + 1e-06)
    vectors = (w2 / (spread1 * spread2)).astype(bf16)
    return (vectors, jnp.stack([spread1, spread2]))


def solution(mesh):
    torus = Mesh(mesh.devices.reshape(4, 4, 16, 2), EVERY)
    placed = (P(GX, GY, None, None), P(GX, GY), P(GX, GY), P(GX, None))
    return jax.shard_map(
        on_device,
        mesh=torus,
        in_specs=placed,
        out_specs=(P(EVERY, None), P()),
        check_vma=False,
    )
```

```python
import functools

import jax
import jax.numpy as jnp
from jax import lax
from jax.experimental import pallas as pl
from jax.experimental.pallas import tpu as pltpu
from jax.sharding import Mesh
from jax.sharding import PartitionSpec as P

GX = ("gx_0", "gx_1")
GY = ("gy_0", "gy_1")
EVERY = ("gx_0", "gx_1", "gy_0", "gy_1")
Z = "gy_0"
CORE = "gy_1"
PLANE = ("gx_0", "gx_1", "gy_1")


def exchange(array, axis):
    return lax.all_to_all(array, axis, 0, 0, tiled=True)


def from_everyone(array, axis):
    peers = lax.axis_size(axis)
    return exchange(jnp.broadcast_to(array[None], (peers, *array.shape)), axis)


def row_sum_kernel(counts, start, tiles, out, sent, held, arrived):
    here, slots, side, _ = tiles.shape
    groups, rows, _ = sent.shape
    share = start.shape[1]
    half = pl.program_id(0)
    copy = pltpu.make_async_copy(
        start.at[pl.ds(lax.axis_index(CORE) * groups, groups)],
        sent.at[:, pl.ds(0, share), :],
        arrived,
    )

    @pl.when(half == 0)
    def _():
        copy.start()

    mine = lax.broadcasted_iota(jnp.int32, (1, side), 1) // share == half
    row = lax.broadcasted_iota(jnp.int32, (rows - share, side), 0)
    ones = jnp.ones((side, side), tiles.dtype)
    down = lax.broadcasted_iota(jnp.int32, (side, side), 0)
    across = lax.broadcasted_iota(jnp.int32, (side, side), 1)
    for t in range(here):
        which = lax.broadcasted_iota(jnp.int32, counts.shape, 1) == half * here + t
        count = jnp.sum(jnp.where(which, counts[...], 0), axis=1, keepdims=True)
        total = jnp.zeros((side, side), jnp.float32)
        for s in range(slots):
            part = jnp.dot(tiles[t, s], ones, preferred_element_type=jnp.float32)
            total = total + jnp.where(s < count, part, 0.0)
        sums = jnp.sum(jnp.where(down == across, total, 0.0), axis=0, keepdims=True)
        out[pl.ds(half * here + t, 1)] = sums
        turned = pltpu.roll(sums, share, 1)
        for part in range(2):
            at = pl.ds(2 * t + part, 1)
            held[at] = jnp.where(
                mine, jnp.where(half == part, sums, turned), held[at]
            )

    @pl.when(half == 1)
    def _():
        for p in range(2 * here):
            value = held[p : p + 1]
            high = value.astype(sent.dtype).astype(jnp.float32)
            middle = (value - high).astype(sent.dtype).astype(jnp.float32)
            low = value - high - middle
            block = jnp.where(row == 1, middle, jnp.where(row == 2, low, 0.0))
            sent[p, share:] = jnp.where(row == 0, high, block).astype(sent.dtype)
        copy.wait()


def spread_kernel(terms, own, out):
    for p in range(terms.shape[0]):
        part = jnp.sum(terms[p].astype(jnp.float32), axis=0, keepdims=True)
        line = jnp.concatenate([part, own[p : p + 1]], axis=1)
        out[2 * p] = line
        out[2 * p + 1] = line


def pick(cols, counts, column, r, slots, side):
    parts = []
    for s in range(slots):
        start = pl.multiple_of(cols[s, r] * side, side)
        part = column[pl.ds(start, side), :]
        live = s < counts[0, r]
        parts.append(jnp.where(live, part, jnp.zeros_like(part)))
    return jnp.concatenate(parts, axis=0)


def first_kernel(flip, place, cols, counts, tiles, column, out):
    row_tiles, slots, side, _ = tiles.shape
    half = row_tiles // 2
    core = 1 - place[0] if flip else place[0]
    for t in range(half):
        r = core * half + t
        wide = jnp.concatenate([tiles[r, s] for s in range(slots)], axis=1)
        out[t * side : (t + 1) * side, :] = jnp.dot(
            wide,
            pick(cols, counts, column, r, slots, side),
            preferred_element_type=jnp.float32,
        ).astype(out.dtype)


def second_kernel(flip, place, cols, counts, tiles, column, out):
    row_tiles, slots, side, _ = tiles.shape
    half = row_tiles // 2
    share = side // 2
    part = 1 - place[0] if flip else place[0]
    rows = pl.ds(pl.multiple_of(part * share, share), share)
    for r in range(row_tiles):
        picked = pick(cols, counts, column, r, slots, side)
        diagonal = (place[1] == place[2]) & (place[0] == r // half)
        wide = jnp.concatenate([tiles[r, s, rows, :] for s in range(slots)], axis=1)
        own = column[pl.ds((r % half) * side + part * share, share), :]
        value = jnp.dot(wide, picked, preferred_element_type=jnp.float32)
        value = value + jnp.where(diagonal, own.astype(jnp.float32), 0.0)
        out[r * share : (r + 1) * share, :] = value.astype(out.dtype)


SMEM = pl.BlockSpec(memory_space=pltpu.SMEM)
VMEM = pl.BlockSpec(memory_space=pltpu.VMEM)
PARAMS = pltpu.CompilerParams(vmem_limit_bytes=24 << 20)
COST = pl.CostEstimate(flops=800 << 20, bytes_accessed=2 << 20, transcendentals=0)


def on_device(tiles, tile_cols, row_counts, start_block):
    row_tiles, slot_count, side, _ = tiles.shape
    width = start_block.shape[1]
    groups = lax.axis_size(GX)
    half_tiles = row_tiles // 2
    local_rows = row_tiles * side
    half_rows = local_rows // 2
    share = half_rows // groups
    nodes = local_rows * groups
    core = lax.axis_index(CORE)
    line = lax.axis_index(GX)
    plane = lax.axis_index(Z)
    f32, bf16 = jnp.float32, jnp.bfloat16

    place = jnp.stack([core, line, plane]).astype(jnp.int32)
    cols = tile_cols.T
    counts = row_counts.T
    steps = 2
    row_sums, sent = pl.pallas_call(
        row_sum_kernel,
        grid=(steps,),
        out_shape=[
            jax.ShapeDtypeStruct((row_tiles, side), f32),
            jax.ShapeDtypeStruct((groups, share + 16, side), bf16),
        ],
        in_specs=[
            pl.BlockSpec((1, row_tiles), lambda g: (0, 0)),
            pl.BlockSpec(memory_space=pl.ANY),
            pl.BlockSpec(
                (row_tiles // steps, slot_count, side, side), lambda g: (g, 0, 0, 0)
            ),
        ],
        out_specs=[pl.BlockSpec((row_tiles, side), lambda g: (0, 0)), VMEM],
        scratch_shapes=[
            pltpu.VMEM((groups, side), f32),
            pltpu.SemaphoreType.DMA(()),
        ],
    )(counts, start_block.reshape(2 * groups, share, width), tiles)

    def swapped(array):
        return lax.ppermute(array, CORE, [(0, 1), (1, 0)])

    at_seg = core * share
    at_own = side + at_seg
    sent, place, at_seg, at_own = lax.optimization_barrier((sent, place, at_seg, at_own))
    got = exchange(sent, GX)
    start_seg = lax.dynamic_index_in_dim(got, plane, 0, keepdims=False)[:share]

    both = pl.pallas_call(
        spread_kernel,
        grid=(1,),
        out_shape=jax.ShapeDtypeStruct((2 * groups, 1, 2 * side), f32),
        in_specs=[
            pl.BlockSpec((groups, 16, side), lambda g: (0, share // 16, 0)),
            VMEM,
        ],
        out_specs=VMEM,
        compiler_params=PARAMS,
    )(got, row_sums)
    degree = 1.0 + exchange(both, GY).sum(axis=(0, 1))
    scale = 1.0 / jnp.sqrt(degree)
    scale_seg = lax.dynamic_slice_in_dim(scale, at_seg, share, 0)
    scale_own = lax.dynamic_slice_in_dim(scale, at_own, share, 0)

    def pair_sum(kernel, column):
        def products(flip, kind):
            return pl.pallas_call(
                functools.partial(kernel, flip),
                out_shape=jax.ShapeDtypeStruct((half_rows, width), kind),
                in_specs=[SMEM] * 3 + [VMEM] * 2,
                out_specs=VMEM,
                compiler_params=PARAMS,
                cost_estimate=COST,
            )(place, cols, counts, tiles, column)

        arrived = swapped(products(True, bf16))
        return products(False, f32) + arrived.astype(f32)

    u_seg = (scale_seg[:, None] * start_seg.astype(f32)).astype(bf16)
    u = from_everyone(u_seg, GX).reshape(half_rows, width)
    pair = pair_sum(first_kernel, u)
    chunks = pair.astype(bf16).reshape(groups, share, width)
    product = exchange(exchange(chunks, GX), Z).astype(f32).sum(axis=0)
    w1 = scale_seg[:, None] * (product + u_seg.astype(f32))
    squares1 = jnp.sum(w1 * w1, axis=0)

    v_seg = (scale_seg[:, None] * w1).astype(bf16)
    v_seg, squares1, scale_own = lax.optimization_barrier((v_seg, squares1, scale_own))
    v = from_everyone(v_seg, GX).reshape(half_rows, width)
    pair = pair_sum(second_kernel, v).reshape(row_tiles, share, width)
    product = exchange(pair.astype(bf16), Z).astype(f32).sum(axis=0)
    w2 = scale_own[:, None] * product
    squares2 = jnp.sum(w2 * w2, axis=0)

    squares = jnp.stack([squares1, squares2])
    squares = from_everyone(squares, PLANE).sum(axis=0)
    squares = from_everyone(squares, Z).sum(axis=0)
    spread1 = jnp.sqrt(squares[0] / nodes + 1e-06)
    spread2 = jnp.sqrt(squares[1] / (spread1 * spread1) / nodes + 1e-06)
    vectors = (w2 / (spread1 * spread2)).astype(bf16)
    return (vectors, jnp.stack([spread1, spread2]))


def solution(mesh):
    torus = Mesh(mesh.devices.reshape(4, 4, 16, 2), EVERY)
    placed = (P(GX, GY, None, None), P(GX, GY), P(GX, GY), P(GX, None))
    return jax.shard_map(
        on_device,
        mesh=torus,
        in_specs=placed,
        out_specs=(P(EVERY, None), P()),
        check_vma=False,
    )
```

```python
import functools

import jax
import jax.numpy as jnp
from jax import lax
from jax.experimental import pallas as pl
from jax.experimental.pallas import tpu as pltpu
from jax.sharding import Mesh
from jax.sharding import PartitionSpec as P

GX = ("gx_0", "gx_1")
GY = ("gy_0", "gy_1")
EVERY = ("gx_0", "gx_1", "gy_0", "gy_1")
Z = "gy_0"
CORE = "gy_1"
PLANE = ("gx_0", "gx_1", "gy_1")


def exchange(array, axis):
    return lax.all_to_all(array, axis, 0, 0, tiled=True)


def from_everyone(array, axis):
    peers = lax.axis_size(axis)
    return exchange(jnp.broadcast_to(array[None], (peers, *array.shape)), axis)


def row_sum_kernel(counts, start, tiles, out, sent, held, arrived):
    here, slots, side, _ = tiles.shape
    groups, rows, _ = sent.shape
    share = start.shape[1]
    half = pl.program_id(0)
    copy = pltpu.make_async_copy(
        start.at[pl.ds(lax.axis_index(CORE) * groups, groups)],
        sent.at[:, pl.ds(0, share), :],
        arrived,
    )

    @pl.when(half == 0)
    def _():
        copy.start()

    mine = lax.broadcasted_iota(jnp.int32, (1, side), 1) // share == half
    row = lax.broadcasted_iota(jnp.int32, (rows - share, side), 0)
    ones = jnp.ones((side, side), tiles.dtype)
    down = lax.broadcasted_iota(jnp.int32, (side, side), 0)
    across = lax.broadcasted_iota(jnp.int32, (side, side), 1)
    for t in range(here):
        which = lax.broadcasted_iota(jnp.int32, counts.shape, 1) == half * here + t
        count = jnp.sum(jnp.where(which, counts[...], 0), axis=1, keepdims=True)
        total = jnp.zeros((side, side), jnp.float32)
        for s in range(slots):
            part = jnp.dot(tiles[t, s], ones, preferred_element_type=jnp.float32)
            total = total + jnp.where(s < count, part, 0.0)
        sums = jnp.sum(jnp.where(down == across, total, 0.0), axis=0, keepdims=True)
        out[pl.ds(half * here + t, 1)] = sums
        turned = pltpu.roll(sums, share, 1)
        for part in range(2):
            at = pl.ds(2 * t + part, 1)
            held[at] = jnp.where(
                mine, jnp.where(half == part, sums, turned), held[at]
            )

    @pl.when(half == 1)
    def _():
        for p in range(2 * here):
            value = held[p : p + 1]
            high = value.astype(sent.dtype).astype(jnp.float32)
            middle = (value - high).astype(sent.dtype).astype(jnp.float32)
            low = value - high - middle
            block = jnp.where(row == 1, middle, jnp.where(row == 2, low, 0.0))
            sent[p, share:] = jnp.where(row == 0, high, block).astype(sent.dtype)
        copy.wait()


def spread_kernel(terms, own, out):
    for p in range(terms.shape[0]):
        part = jnp.sum(terms[p].astype(jnp.float32), axis=0, keepdims=True)
        line = jnp.concatenate([part, own[p : p + 1]], axis=1)
        out[2 * p] = line
        out[2 * p + 1] = line


def pick(cols, counts, column, r, slots, side):
    parts = []
    for s in range(slots):
        start = pl.multiple_of(cols[s, r] * side, side)
        part = column[pl.ds(start, side), :]
        live = s < counts[0, r]
        parts.append(jnp.where(live, part, jnp.zeros_like(part)))
    return jnp.concatenate(parts, axis=0)


def first_kernel(flip, place, cols, counts, tiles, column, out):
    row_tiles, slots, side, _ = tiles.shape
    half = row_tiles // 2
    core = 1 - place[0] if flip else place[0]
    for t in range(half):
        r = core * half + t
        wide = jnp.concatenate([tiles[r, s] for s in range(slots)], axis=1)
        out[t * side : (t + 1) * side, :] = jnp.dot(
            wide,
            pick(cols, counts, column, r, slots, side),
            preferred_element_type=jnp.float32,
        ).astype(out.dtype)


def second_kernel(flip, place, cols, counts, tiles, column, out):
    row_tiles, slots, side, _ = tiles.shape
    half = row_tiles // 2
    share = side // 2
    part = 1 - place[0] if flip else place[0]
    rows = pl.ds(pl.multiple_of(part * share, share), share)
    for r in range(row_tiles):
        picked = pick(cols, counts, column, r, slots, side)
        diagonal = (place[1] == place[2]) & (place[0] == r // half)
        wide = jnp.concatenate([tiles[r, s, rows, :] for s in range(slots)], axis=1)
        own = column[pl.ds((r % half) * side + part * share, share), :]
        value = jnp.dot(wide, picked, preferred_element_type=jnp.float32)
        value = value + jnp.where(diagonal, own.astype(jnp.float32), 0.0)
        out[r * share : (r + 1) * share, :] = value.astype(out.dtype)


def last_kernel(nodes, squares, w2, vectors, spreads):
    total = jnp.sum(squares[...], axis=0)
    first = jnp.sqrt(total[0:1] / nodes + 1e-06)
    second = jnp.sqrt(total[1:2] / (first * first) / nodes + 1e-06)
    vectors[...] = (w2[...] / (first * second)).astype(vectors.dtype)
    spreads[0:1] = first
    spreads[1:2] = second


SMEM = pl.BlockSpec(memory_space=pltpu.SMEM)
VMEM = pl.BlockSpec(memory_space=pltpu.VMEM)
PARAMS = pltpu.CompilerParams(vmem_limit_bytes=24 << 20)
COST = pl.CostEstimate(flops=800 << 20, bytes_accessed=2 << 20, transcendentals=0)


def on_device(tiles, tile_cols, row_counts, start_block):
    row_tiles, slot_count, side, _ = tiles.shape
    width = start_block.shape[1]
    groups = lax.axis_size(GX)
    half_tiles = row_tiles // 2
    local_rows = row_tiles * side
    half_rows = local_rows // 2
    share = half_rows // groups
    nodes = local_rows * groups
    core = lax.axis_index(CORE)
    line = lax.axis_index(GX)
    plane = lax.axis_index(Z)
    f32, bf16 = jnp.float32, jnp.bfloat16

    place = jnp.stack([core, line, plane]).astype(jnp.int32)
    cols = tile_cols.T
    counts = row_counts.T
    steps = 2
    row_sums, sent = pl.pallas_call(
        row_sum_kernel,
        grid=(steps,),
        out_shape=[
            jax.ShapeDtypeStruct((row_tiles, side), f32),
            jax.ShapeDtypeStruct((groups, share + 16, side), bf16),
        ],
        in_specs=[
            pl.BlockSpec((1, row_tiles), lambda g: (0, 0)),
            pl.BlockSpec(memory_space=pl.ANY),
            pl.BlockSpec(
                (row_tiles // steps, slot_count, side, side), lambda g: (g, 0, 0, 0)
            ),
        ],
        out_specs=[pl.BlockSpec((row_tiles, side), lambda g: (0, 0)), VMEM],
        scratch_shapes=[
            pltpu.VMEM((groups, side), f32),
            pltpu.SemaphoreType.DMA(()),
        ],
    )(counts, start_block.reshape(2 * groups, share, width), tiles)

    def swapped(array):
        return lax.ppermute(array, CORE, [(0, 1), (1, 0)])

    at_seg = core * share
    at_own = side + at_seg
    sent, place, at_seg, at_own = lax.optimization_barrier((sent, place, at_seg, at_own))
    got = exchange(sent, GX)
    start_seg = lax.dynamic_index_in_dim(got, plane, 0, keepdims=False)[:share]

    both = pl.pallas_call(
        spread_kernel,
        grid=(1,),
        out_shape=jax.ShapeDtypeStruct((2 * groups, 1, 2 * side), f32),
        in_specs=[
            pl.BlockSpec((groups, 16, side), lambda g: (0, share // 16, 0)),
            VMEM,
        ],
        out_specs=VMEM,
        compiler_params=PARAMS,
    )(got, row_sums)
    degree = 1.0 + exchange(both, GY).sum(axis=(0, 1))
    scale = 1.0 / jnp.sqrt(degree)
    scale_seg = lax.dynamic_slice_in_dim(scale, at_seg, share, 0)
    scale_own = lax.dynamic_slice_in_dim(scale, at_own, share, 0)

    def pair_sum(kernel, column):
        def products(flip, kind):
            return pl.pallas_call(
                functools.partial(kernel, flip),
                out_shape=jax.ShapeDtypeStruct((half_rows, width), kind),
                in_specs=[SMEM] * 3 + [VMEM] * 2,
                out_specs=VMEM,
                compiler_params=PARAMS,
                cost_estimate=COST,
            )(place, cols, counts, tiles, column)

        arrived = swapped(products(True, bf16))
        return products(False, f32) + arrived.astype(f32)

    u_seg = (scale_seg[:, None] * start_seg.astype(f32)).astype(bf16)
    u = from_everyone(u_seg, GX).reshape(half_rows, width)
    pair = pair_sum(first_kernel, u)
    chunks = pair.astype(bf16).reshape(groups, share, width)
    product = exchange(exchange(chunks, GX), Z).astype(f32).sum(axis=0)
    w1 = scale_seg[:, None] * (product + u_seg.astype(f32))
    squares1 = jnp.sum(w1 * w1, axis=0)

    v_seg = (scale_seg[:, None] * w1).astype(bf16)
    v_seg, squares1, scale_own = lax.optimization_barrier((v_seg, squares1, scale_own))
    v = from_everyone(v_seg, GX).reshape(half_rows, width)
    pair = pair_sum(second_kernel, v).reshape(row_tiles, share, width)
    product = exchange(pair.astype(bf16), Z).astype(f32).sum(axis=0)
    w2 = scale_own[:, None] * product
    squares2 = jnp.sum(w2 * w2, axis=0)

    squares = jnp.stack([squares1, squares2])
    squares = from_everyone(squares, PLANE).sum(axis=0)
    return tuple(
        pl.pallas_call(
            functools.partial(last_kernel, nodes),
            out_shape=[
                jax.ShapeDtypeStruct((share, width), bf16),
                jax.ShapeDtypeStruct((2, width), f32),
            ],
            in_specs=[VMEM] * 2,
            out_specs=[VMEM] * 2,
            compiler_params=PARAMS,
        )(from_everyone(squares, Z), w2)
    )


def solution(mesh):
    torus = Mesh(mesh.devices.reshape(4, 4, 16, 2), EVERY)
    placed = (P(GX, GY, None, None), P(GX, GY), P(GX, GY), P(GX, None))
    return jax.shard_map(
        on_device,
        mesh=torus,
        in_specs=placed,
        out_specs=(P(EVERY, None), P()),
        check_vma=False,
    )
```

```python
import functools

import jax
import jax.numpy as jnp
from jax import lax
from jax.experimental import pallas as pl
from jax.experimental.pallas import tpu as pltpu
from jax.sharding import Mesh
from jax.sharding import PartitionSpec as P

GX = ("gx_0", "gx_1")
GY = ("gy_0", "gy_1")
EVERY = ("gx_0", "gx_1", "gy_0", "gy_1")
Z = "gy_0"
CORE = "gy_1"
PLANE = ("gx_0", "gx_1", "gy_1")


def exchange(array, axis):
    return lax.all_to_all(array, axis, 0, 0, tiled=True)


def from_everyone(array, axis):
    peers = lax.axis_size(axis)
    return exchange(jnp.broadcast_to(array[None], (peers, *array.shape)), axis)


def row_sum_kernel(counts, start, tiles, out, sent, held, arrived):
    here, slots, side, _ = tiles.shape
    groups, rows, _ = sent.shape
    share = start.shape[1]
    half = pl.program_id(0)
    copy = pltpu.make_async_copy(
        start.at[pl.ds(lax.axis_index(CORE) * groups, groups)],
        sent.at[:, pl.ds(0, share), :],
        arrived,
    )

    @pl.when(half == 0)
    def _():
        copy.start()

    mine = lax.broadcasted_iota(jnp.int32, (1, side), 1) // share == half
    row = lax.broadcasted_iota(jnp.int32, (rows - share, side), 0)
    ones = jnp.ones((side, side), tiles.dtype)
    down = lax.broadcasted_iota(jnp.int32, (side, side), 0)
    across = lax.broadcasted_iota(jnp.int32, (side, side), 1)
    for t in range(here):
        which = lax.broadcasted_iota(jnp.int32, counts.shape, 1) == half * here + t
        count = jnp.sum(jnp.where(which, counts[...], 0), axis=1, keepdims=True)
        total = jnp.zeros((side, side), jnp.float32)
        for s in range(slots):
            part = jnp.dot(tiles[t, s], ones, preferred_element_type=jnp.float32)
            total = total + jnp.where(s < count, part, 0.0)
        sums = jnp.sum(jnp.where(down == across, total, 0.0), axis=0, keepdims=True)
        out[pl.ds(half * here + t, 1)] = sums
        turned = pltpu.roll(sums, share, 1)
        for part in range(2):
            at = pl.ds(2 * t + part, 1)
            held[at] = jnp.where(
                mine, jnp.where(half == part, sums, turned), held[at]
            )

    @pl.when(half == 1)
    def _():
        for p in range(2 * here):
            value = held[p : p + 1]
            high = value.astype(sent.dtype).astype(jnp.float32)
            middle = (value - high).astype(sent.dtype).astype(jnp.float32)
            low = value - high - middle
            block = jnp.where(row == 1, middle, jnp.where(row == 2, low, 0.0))
            sent[p, share:] = jnp.where(row == 0, high, block).astype(sent.dtype)
        copy.wait()


def spread_kernel(terms, own, out):
    for p in range(terms.shape[0]):
        part = jnp.sum(terms[p].astype(jnp.float32), axis=0, keepdims=True)
        line = jnp.concatenate([part, own[p : p + 1]], axis=1)
        out[2 * p] = line
        out[2 * p + 1] = line


def pick(cols, counts, column, r, slots, side):
    parts = []
    for s in range(slots):
        start = pl.multiple_of(cols[s, r] * side, side)
        part = column[pl.ds(start, side), :]
        live = s < counts[0, r]
        parts.append(jnp.where(live, part, jnp.zeros_like(part)))
    return jnp.concatenate(parts, axis=0)


def first_kernel(flip, place, cols, counts, tiles, column, out):
    row_tiles, slots, side, _ = tiles.shape
    half = row_tiles // 2
    core = 1 - place[0] if flip else place[0]
    for t in range(half):
        r = core * half + t
        wide = jnp.concatenate([tiles[r, s] for s in range(slots)], axis=1)
        out[t * side : (t + 1) * side, :] = jnp.dot(
            wide,
            pick(cols, counts, column, r, slots, side),
            preferred_element_type=jnp.float32,
        ).astype(out.dtype)


def second_kernel(flip, place, cols, counts, tiles, column, out):
    row_tiles, slots, side, _ = tiles.shape
    half = row_tiles // 2
    share = side // 2
    part = 1 - place[0] if flip else place[0]
    rows = pl.ds(pl.multiple_of(part * share, share), share)
    for r in range(row_tiles):
        picked = pick(cols, counts, column, r, slots, side)
        diagonal = (place[1] == place[2]) & (place[0] == r // half)
        wide = jnp.concatenate([tiles[r, s, rows, :] for s in range(slots)], axis=1)
        own = column[pl.ds((r % half) * side + part * share, share), :]
        value = jnp.dot(wide, picked, preferred_element_type=jnp.float32)
        value = value + jnp.where(diagonal, own.astype(jnp.float32), 0.0)
        out[r * share : (r + 1) * share, :] = value.astype(out.dtype)


def last_kernel(nodes, squares, w2, vectors, spreads):
    total = jnp.sum(squares[...], axis=0)
    first = jnp.sqrt(total[0:1] / nodes + 1e-06)
    second = jnp.sqrt(total[1:2] / (first * first) / nodes + 1e-06)
    vectors[...] = (w2[...] / (first * second)).astype(vectors.dtype)
    spreads[0:1] = first
    spreads[1:2] = second


SMEM = pl.BlockSpec(memory_space=pltpu.SMEM)
VMEM = pl.BlockSpec(memory_space=pltpu.VMEM)
PARAMS = pltpu.CompilerParams(vmem_limit_bytes=24 << 20)
COST = pl.CostEstimate(flops=800 << 20, bytes_accessed=2 << 20, transcendentals=0)


def on_device(tiles, tile_cols, row_counts, start_block):
    row_tiles, slot_count, side, _ = tiles.shape
    width = start_block.shape[1]
    groups = lax.axis_size(GX)
    half_tiles = row_tiles // 2
    local_rows = row_tiles * side
    half_rows = local_rows // 2
    share = half_rows // groups
    nodes = local_rows * groups
    core = lax.axis_index(CORE)
    line = lax.axis_index(GX)
    plane = lax.axis_index(Z)
    f32, bf16 = jnp.float32, jnp.bfloat16

    place = jnp.stack([core, line, plane]).astype(jnp.int32)
    cols = tile_cols.T
    counts = row_counts.T
    steps = 2
    row_sums, sent = pl.pallas_call(
        row_sum_kernel,
        grid=(steps,),
        out_shape=[
            jax.ShapeDtypeStruct((row_tiles, side), f32),
            jax.ShapeDtypeStruct((groups, share + 16, side), bf16),
        ],
        in_specs=[
            pl.BlockSpec((1, row_tiles), lambda g: (0, 0)),
            pl.BlockSpec(memory_space=pl.ANY),
            pl.BlockSpec(
                (row_tiles // steps, slot_count, side, side), lambda g: (g, 0, 0, 0)
            ),
        ],
        out_specs=[VMEM] * 2,
        compiler_params=pltpu.CompilerParams(vmem_limit_bytes=63 << 20),
        scratch_shapes=[
            pltpu.VMEM((groups, side), f32),
            pltpu.SemaphoreType.DMA(()),
        ],
    )(counts, start_block.reshape(2 * groups, share, width), tiles)

    def swapped(array):
        return lax.ppermute(array, CORE, [(0, 1), (1, 0)])

    at_seg = core * share
    at_own = side + at_seg
    sent, place, at_seg, at_own = lax.optimization_barrier((sent, place, at_seg, at_own))
    got = exchange(sent, GX)
    start_seg = lax.dynamic_index_in_dim(got, plane, 0, keepdims=False)[:share]

    both = pl.pallas_call(
        spread_kernel,
        grid=(1,),
        out_shape=jax.ShapeDtypeStruct((2 * groups, 1, 2 * side), f32),
        in_specs=[
            pl.BlockSpec((groups, 16, side), lambda g: (0, share // 16, 0)),
            VMEM,
        ],
        out_specs=VMEM,
        compiler_params=PARAMS,
    )(got, row_sums)
    degree = 1.0 + exchange(both, GY).sum(axis=(0, 1))
    scale = 1.0 / jnp.sqrt(degree)
    scale_seg = lax.dynamic_slice_in_dim(scale, at_seg, share, 0)
    scale_own = lax.dynamic_slice_in_dim(scale, at_own, share, 0)

    def pair_sum(kernel, column):
        def products(flip, kind):
            return pl.pallas_call(
                functools.partial(kernel, flip),
                out_shape=jax.ShapeDtypeStruct((half_rows, width), kind),
                in_specs=[SMEM] * 3 + [VMEM] * 2,
                out_specs=VMEM,
                compiler_params=PARAMS,
                cost_estimate=COST,
            )(place, cols, counts, tiles, column)

        arrived = swapped(products(True, bf16))
        return products(False, f32) + arrived.astype(f32)

    u_seg = (scale_seg[:, None] * start_seg.astype(f32)).astype(bf16)
    u = from_everyone(u_seg, GX).reshape(half_rows, width)
    pair = pair_sum(first_kernel, u)
    chunks = pair.astype(bf16).reshape(groups, share, width)
    product = exchange(exchange(chunks, GX), Z).astype(f32).sum(axis=0)
    w1 = scale_seg[:, None] * (product + u_seg.astype(f32))
    squares1 = jnp.sum(w1 * w1, axis=0)

    v_seg = (scale_seg[:, None] * w1).astype(bf16)
    v_seg, squares1, scale_own = lax.optimization_barrier((v_seg, squares1, scale_own))
    v = from_everyone(v_seg, GX).reshape(half_rows, width)
    pair = pair_sum(second_kernel, v).reshape(row_tiles, share, width)
    product = exchange(pair.astype(bf16), Z).astype(f32).sum(axis=0)
    w2 = scale_own[:, None] * product
    squares2 = jnp.sum(w2 * w2, axis=0)

    squares = jnp.stack([squares1, squares2])
    squares = from_everyone(squares, PLANE).sum(axis=0)
    return tuple(
        pl.pallas_call(
            functools.partial(last_kernel, nodes),
            out_shape=[
                jax.ShapeDtypeStruct((share, width), bf16),
                jax.ShapeDtypeStruct((2, width), f32),
            ],
            in_specs=[VMEM] * 2,
            out_specs=[VMEM] * 2,
            compiler_params=PARAMS,
        )(from_everyone(squares, Z), w2)
    )


def solution(mesh):
    torus = Mesh(mesh.devices.reshape(4, 4, 16, 2), EVERY)
    placed = (P(GX, GY, None, None), P(GX, GY), P(GX, GY), P(GX, None))
    return jax.shard_map(
        on_device,
        mesh=torus,
        in_specs=placed,
        out_specs=(P(EVERY, None), P()),
        check_vma=False,
    )
```
